256 devices in a mesh: band: 64 (over x, z, core), lev: 4 (over y).
Axes of the slice: x: 4, y: 4, z: 8, core: 2. Of those that a mesh axis runs over, the one named last changes fastest.
Arguments:
- fields: bfloat16 [8, 136, 65536], P(None, 'lev', 'band'), may hold values from -6 to 6
- depart: int32 [136, 65536], P('lev', 'band'), may hold values from -512 to -1
- fraction: bfloat16 [2, 136, 65536], P(None, 'lev', 'band'), may hold values from 0 to 1
- w_first: bfloat16 [8, 136, 256], replicated, may hold values from -0.1875 to 0.1875
- b_first: float32 [256], replicated, may hold values from -4 to 4
- w_middle: bfloat16 [256, 256], replicated, may hold values from -0.375 to 0.375
- b_middle: float32 [256], replicated, may hold values from -4 to 4
- w_last: bfloat16 [8, 136, 256], replicated, may hold values from -0.375 to 0.375
Outputs:
- updated: bfloat16 [8, 136, 65536], P(None, 'lev', 'band')
The draws below stay inside these ranges and needn't reach their ends.
Inputs may be any that keep to these rules, and one draw needn't show every extreme that they name: The departure corner of arrival column c is column c + depart, counted around the cycle of 65536 columns.
All inputs are finite; a program needn't handle non-finite values.
Results may differ from the reference program's by a relative error of at most 0.0053.
Values may be sent and summed in bfloat16 or wider, within the bound.
A program may use at most 64 MiB of HBM per device.

```python
import math
import jax
import jax.numpy as jnp
from jax import lax

FIELDS = 8
LEVELS = 136
HIDDEN_SIZE = 256
ROW = 512
NCOL = 65536


def touch_ends(entries, stream_key, least, high):
    dims = entries.shape
    place = [jax.random.randint(jax.random.fold_in(stream_key, axis), (), 0, dims[axis]) for axis in range(len(dims))]
    entries = entries.at[tuple(place)].set(least)
    longest = dims.index(max(dims))
    place[longest] = (place[longest] + 1) % dims[longest]
    return entries.at[tuple(place)].set(high)


def block_levels(stream_key, dims, split, smallest, largest):
    loudness = 1.0
    for dim, blocks in split:
        heights = jax.random.uniform(jax.random.fold_in(jax.random.fold_in(stream_key, 6), dim), (blocks,), jnp.float32, smallest / len(split), largest / len(split))
        loudness = loudness * jnp.repeat(jnp.exp(heights), dims[dim] // blocks).reshape((-1,) + (1,) * (len(dims) - 1 - dim))
    return loudness


def centred(own_key, extent, scale, most, shards=(), kind=jnp.bfloat16):
    result = scale * jax.random.normal(own_key, extent, jnp.float32)
    if shards:
        result = result * block_levels(own_key, extent, shards, -0.22, 0.18)
    return jnp.clip(result, -most, most).astype(kind)


def setup_inputs(seed: int = 0) -> dict:
    arg_keys = jax.random.split(jax.random.key(seed), 9)
    fields = centred(arg_keys[0], (FIELDS, LEVELS, NCOL), 1.0, 6.0, ((1, 4), (2, 64)))
    depart = touch_ends(jax.random.randint(arg_keys[1], (LEVELS, NCOL), 0 - ROW, 0), jax.random.fold_in(arg_keys[1], 1), 0 - ROW, -1).astype(jnp.int32)
    fraction = jnp.clip(1.0 * jax.random.uniform(arg_keys[2], (2, LEVELS, NCOL), jnp.float32) ** block_levels(arg_keys[2], (2, LEVELS, NCOL), ((1, 4), (2, 64)), -0.2, 0.2), 0.0, 1.0).astype(jnp.bfloat16)
    w_first = centred(arg_keys[3], (FIELDS, LEVELS, HIDDEN_SIZE), (FIELDS * LEVELS) ** -0.5, 0.1875)
    b_first = centred(arg_keys[4], (HIDDEN_SIZE,), 1.0, 4.0, (), jnp.float32)
    w_middle = centred(arg_keys[5], (HIDDEN_SIZE, HIDDEN_SIZE), HIDDEN_SIZE ** -0.5, 0.375)
    b_middle = centred(arg_keys[6], (HIDDEN_SIZE,), 1.0, 4.0, (), jnp.float32)
    w_last = centred(arg_keys[7], (FIELDS, LEVELS, HIDDEN_SIZE), HIDDEN_SIZE ** -0.5, 0.375)
    return {"fields": fields, "depart": depart, "fraction": fraction, "w_first": w_first, "b_first": b_first, "w_middle": w_middle, "b_middle": b_middle, "w_last": w_last}


def interpolate(fields, depart, fraction):
    ncol = fields.shape[2]
    column = jnp.arange(ncol, dtype=jnp.int32)
    corner = column[None, :] + depart
    along = fraction[0].astype(jnp.float32)
    across = fraction[1].astype(jnp.float32)
    weights = ((1.0 - along) * (1.0 - across), along * (1.0 - across), (1.0 - along) * across, along * across)
    offsets = (0, 1, ROW, ROW + 1)

    def one_field(field):
        total = jnp.zeros(field.shape, jnp.float32)
        for weight, offset in zip(weights, offsets):
            where = jnp.mod(corner + offset, ncol).astype(jnp.int32)
            total = total + weight * jnp.take_along_axis(field, where, axis=1).astype(jnp.float32)
        return total.astype(jnp.bfloat16)

    return lax.map(one_field, fields)


def reference(fields, depart, fraction, w_first, b_first, w_middle, b_middle, w_last):
    advected = interpolate(fields, depart, fraction)
    ncol = advected.shape[2]
    width = math.gcd(ncol, 4096)
    blocks = advected.reshape(FIELDS, LEVELS, ncol // width, width).transpose(2, 0, 1, 3)

    def physics(block):
        first = jnp.einsum("flh,flc->hc", w_first.astype(jnp.float32), block.astype(jnp.float32)) + b_first[:, None]
        first = jax.nn.silu(first).astype(jnp.bfloat16)
        middle = jnp.dot(w_middle.T, first, preferred_element_type=jnp.float32) + b_middle[:, None]
        middle = jax.nn.silu(middle).astype(jnp.bfloat16)
        tendency = jnp.einsum("flh,hc->flc", w_last.astype(jnp.float32), middle.astype(jnp.float32))
        return (block.astype(jnp.float32) + tendency).astype(jnp.bfloat16)

    updated = lax.map(physics, blocks)
    return updated.transpose(1, 2, 0, 3).reshape(FIELDS, LEVELS, ncol)
```

```python
import functools

import jax
import jax.numpy as jnp
from jax import lax
from jax.experimental import pallas as pl
from jax.experimental.pallas import tpu as pltpu
from jax.sharding import PartitionSpec as P

MESH = pl.DeviceIdType.MESH
F32, BF16 = jnp.float32, jnp.bfloat16
LANES = 128
ROW = 512

_PICK = lax.GatherDimensionNumbers(
    offset_dims=(),
    collapsed_slice_dims=(1,),
    start_index_map=(1,),
    operand_batching_dims=(0,),
    start_indices_batching_dims=(0,),
)


def lane_gather(x, lane):
    return lax.gather(
        x, lane[..., None], _PICK, (1, 1), mode=lax.GatherScatterMode.PROMISE_IN_BOUNDS
    )


def silu(v):
    return v / (1.0 + jnp.exp(-v))


def kernel(
    nband, nlev, fields, depart, fraction, w_first, w_last, w_middle, b_first, b_middle, out,
    ext, dep_v, frac_v, wf_v, wl_v, wm_v, bf_v, bm_v, p16, w00, w01, w10, w11,
    adv, w1t, w3, w2t, b1, b2, part, opp_tx, opp_rx, near_tx, near_rx, mid, out_v,
    load_sem, halo_send, halo_recv, opp_send, opp_recv, near_send, near_recv,
    mid_send, mid_recv, fwd_send, fwd_recv, store_sem,
):
    band, me = lax.axis_index("band"), lax.axis_index("lev")
    nrow = adv.shape[0]
    levels = nrow // 8
    core = lax.rem(band, 2)
    east, west = lax.rem(band + 1, nband), lax.rem(band + nband - 1, nband)
    up, down, far = lax.rem(me + 1, nlev), lax.rem(me + nlev - 1, nlev), lax.rem(me + 2, nlev)

    barrier = pltpu.get_barrier_semaphore()
    for peer in ({"band": east}, {"band": west}, {"lev": up}, {"lev": down}):
        pl.semaphore_signal(barrier, inc=1, device_id=peer, device_id_type=MESH)

    loads = [
        pltpu.make_async_copy(src, dst, load_sem.at[n])
        for n, (src, dst) in enumerate(
            (
                (depart, dep_v), (fraction, frac_v), (w_first, wf_v), (w_last, wl_v), (w_middle, wm_v),
                (b_first, bf_v), (b_middle, bm_v), (fields, ext.at[:, :, pl.ds(ROW, 2 * ROW)]),
            )
        )
    ]
    for load in loads:
        load.start()
    pl.semaphore_wait(barrier, 4)

    halos = []
    for i in range(4):
        for side, peer, src, dst in ((0, east, 7 - i, 3 - i), (1, west, i, 12 + i)):
            copy = pltpu.make_async_remote_copy(
                src_ref=fields.at[:, :, pl.ds(src * LANES, LANES)],
                dst_ref=ext.at[:, :, pl.ds(dst * LANES, LANES)],
                send_sem=halo_send.at[side, i],
                recv_sem=halo_recv.at[side, i],
                device_id={"band": peer},
                device_id_type=MESH,
            )
            copy.start()
            halos.append(copy)

    loads[0].wait()
    loads[1].wait()

    def prepare(i, carry):
        lane = lax.rem(lax.broadcasted_iota(jnp.int32, (8, 2 * ROW), 1), LANES) + ROW
        where, weights = [], []
        for j in range(2):
            level = 2 * i + j
            where.append(lane + jnp.broadcast_to(dep_v[pl.ds(level, 1), :], (8, 2 * ROW)))
            both = frac_v[level].astype(F32)
            a = jnp.broadcast_to(both[0:1], (8, 2 * ROW))
            b = jnp.broadcast_to(both[1:2], (8, 2 * ROW))
            weights.append(((1.0 - a) * (1.0 - b), a * (1.0 - b), (1.0 - a) * b, a * b))
        rows = pl.ds(pl.multiple_of(16 * i, 16), 16)
        p16[rows, :] = jnp.concatenate(where, axis=0).astype(jnp.int16)
        for ref, one, two in zip((w00, w01, w10, w11), *weights):
            ref[rows, :] = jnp.concatenate([one, two], axis=0)
        return carry

    lax.fori_loop(0, levels // 2, prepare, 0)

    for load in loads[2:7]:
        load.wait()
    total_rows = wf_v.shape[0]
    total_levels = total_rows // 8
    r = lax.broadcasted_iota(jnp.int32, (nrow, total_rows), 0)
    source = lax.rem(r, 8) * total_levels + me * levels + r // 8
    pick = jnp.where(lax.broadcasted_iota(jnp.int32, (nrow, total_rows), 1) == source, 1.0, 0.0).astype(BF16)
    w3[...] = jnp.dot(pick, wl_v[...], preferred_element_type=F32).astype(BF16)
    w1t[...] = jnp.dot(pick, wf_v[...], preferred_element_type=F32).T.astype(BF16)
    w2t[...] = wm_v[...].astype(F32).T.astype(BF16)
    b1[...] = jnp.broadcast_to(bf_v[...], (LANES, bf_v.shape[1])).T
    b2[...] = jnp.broadcast_to(bm_v[...], (LANES, bm_v.shape[1])).T
    loads[7].wait()

    def advect(block):
        base = pl.multiple_of(block * LANES, LANES)
        cols = pl.ds(base, LANES)

        def group(g, carry):
            rows = pl.ds(pl.multiple_of(16 * g, 16), 16)
            p = p16[rows, cols]
            tiles = [
                ext[pl.ds(2 * g, 2), :, pl.ds(base + LANES * t, LANES)].reshape(16, LANES) for t in range(9)
            ]
            total = None
            for off, near, beyond in ((0, w00, w10), (1, w01, w11)):
                q = p + jnp.int16(off)
                lane = q & jnp.int16(LANES - 1)
                masks = [q >= jnp.int16(LANES * j) for j in range(1, 5)]
                got = [lane_gather(t, lane) for t in tiles]
                for start, weight in ((0, near), (4, beyond)):
                    value = got[start]
                    for j in range(4):
                        value = jnp.where(masks[j], got[start + j + 1], value)
                    term = weight[rows, cols] * value.astype(F32)
                    total = term if total is None else total + term
            adv[rows, cols] = total.astype(BF16)
            return carry

        lax.fori_loop(0, nrow // 16, group, 0)
        return cols

    def block_of(half, i):
        right = (1 - core) if half == 0 else core
        return right, right * (4 + i) + (1 - right) * (3 - i)

    def forward(half, i):
        right, block = block_of(half, i)
        tile = right * (12 + i) + (1 - right) * (3 - i)
        pltpu.make_async_remote_copy(
            src_ref=fields.at[:, :, pl.ds(0, LANES)],
            dst_ref=ext.at[:, :, pl.ds(pl.multiple_of(tile * LANES, LANES), LANES)],
            send_sem=halo_send.at[right, i],
            recv_sem=halo_recv.at[right, i],
            device_id={"band": east},
            device_id_type=MESH,
        ).wait_recv()
        cols = advect(block)
        part[half, i] = jnp.dot(w1t[...], adv[:, cols], preferred_element_type=F32)

    def remote(src, dst, send, recv, peer):
        return pltpu.make_async_remote_copy(
            src_ref=src, dst_ref=dst, send_sem=send, recv_sem=recv, device_id={"lev": peer}, device_id_type=MESH
        )

    hidden = w1t.shape[0]
    top, bottom = pl.ds(0, hidden // 2), pl.ds(hidden // 2, hidden // 2)
    sent = []

    def send_far(half):
        opp_tx[half] = part[half, far].astype(BF16)
        for way, rows, peer in ((0, top, up), (1, bottom, down)):
            copy = remote(
                opp_tx.at[half, rows], opp_rx.at[half, way], opp_send.at[half, way], opp_recv.at[half, way], peer
            )
            copy.start()
            sent.append(copy)

    def send_near(half):
        for way, rows, other, peer in ((0, top, bottom, up), (1, bottom, top, down)):
            remote(
                opp_tx.at[half, rows], opp_rx.at[half, way], opp_send.at[half, way], opp_recv.at[half, way], peer
            ).wait_recv()
            near_tx[half, way, rows] = (part[half, peer, rows] + opp_rx[half, way].astype(F32)).astype(BF16)
            near_tx[half, way, other] = part[half, peer, other].astype(BF16)
            copy = remote(
                near_tx.at[half, way], near_rx.at[half, way], near_send.at[half, way], near_recv.at[half, way], peer
            )
            copy.start()
            sent.append(copy)

    def finish(half):
        total = part[half, me] + b1[...]
        for way, peer in ((0, up), (1, down)):
            remote(
                near_tx.at[half, way], near_rx.at[half, way], near_send.at[half, way], near_recv.at[half, way], peer
            ).wait_recv()
            total = total + near_rx[half, way].astype(F32)
        first = silu(total).astype(BF16)
        second = jnp.dot(w2t[...], first, preferred_element_type=F32) + b2[...]
        mid[half, me] = silu(second).astype(BF16)
        for way, peer in ((0, up), (1, down)):
            copy = remote(
                mid.at[half, me], mid.at[half, me], mid_send.at[half, way], mid_recv.at[half, way], peer
            )
            copy.start()
            sent.append(copy)

    def pass_on(half):
        for way, rows, owner, peer in ((0, top, down, up), (1, bottom, up, down)):
            remote(
                mid.at[half, owner], mid.at[half, owner], mid_send.at[half, way], mid_recv.at[half, way], peer
            ).wait_recv()
            copy = remote(
                mid.at[half, owner, rows], mid.at[half, owner, rows],
                fwd_send.at[half, way], fwd_recv.at[half, way], peer,
            )
            copy.start()
            sent.append(copy)

    stores = []

    def last(half, i):
        _, block = block_of(half, i)
        cols = pl.ds(pl.multiple_of(block * LANES, LANES), LANES)
        tendency = jnp.dot(w3[...], mid[half, i], preferred_element_type=F32)
        updated = (adv[:, cols].astype(F32) + tendency).astype(BF16)
        out_v[:, :, cols] = updated.reshape(levels, 8, LANES)
        store = pltpu.make_async_copy(out_v.at[:, :, cols], out.at[:, :, cols], store_sem.at[half, i])
        store.start()
        stores.append(store)

    def finale(half):
        last(half, me)
        last(half, up)
        last(half, down)
        for way, rows, peer in ((0, top, up), (1, bottom, down)):
            remote(
                mid.at[half, far, rows], mid.at[half, far, rows],
                fwd_send.at[half, way], fwd_recv.at[half, way], peer,
            ).wait_recv()
        last(half, far)

    for i in range(4):
        forward(0, i)
    send_far(0)
    forward(1, 0)
    send_near(0)
    forward(1, 1)
    forward(1, 2)
    finish(0)
    forward(1, 3)
    send_far(1)
    pass_on(0)
    send_near(1)
    finale(0)
    finish(1)
    pass_on(1)
    finale(1)

    for copy in halos + sent:
        copy.wait_send()
    for store in stores:
        store.wait()


def on_device(nband, nlev, fields, depart, fraction, w_first, b_first, w_middle, b_middle, w_last):
    nfield, levels, ncols = fields.shape
    nrow, hidden = nfield * levels, w_middle.shape[0]
    V, DMA = pltpu.VMEM, pltpu.SemaphoreType.DMA
    table = V((nrow, ncols), F32)
    whole = V((nfield * w_first.shape[1], hidden), BF16)
    result = pl.pallas_call(
        functools.partial(kernel, nband, nlev),
        out_shape=jax.ShapeDtypeStruct((levels, nfield, ncols), BF16),
        in_specs=[pl.BlockSpec(memory_space=pl.ANY)] * 8,
        out_specs=pl.BlockSpec(memory_space=pl.ANY),
        scratch_shapes=[
            V((levels, nfield, 2 * ncols), BF16),
            V((levels, ncols), jnp.int32),
            V((levels, 2, ncols), BF16),
            whole,
            whole,
            V((hidden, hidden), BF16),
            V((1, hidden), F32),
            V((1, hidden), F32),
            V((nrow, ncols), jnp.int16),
            table, table, table, table,
            V((nrow, ncols), BF16),
            V((hidden, nrow), BF16),
            V((nrow, hidden), BF16),
            V((hidden, hidden), BF16),
            V((hidden, LANES), F32),
            V((hidden, LANES), F32),
            V((2, 4, hidden, LANES), F32),
            V((2, hidden, LANES), BF16),
            V((2, 2, hidden // 2, LANES), BF16),
            V((2, 2, hidden, LANES), BF16),
            V((2, 2, hidden, LANES), BF16),
            V((2, 4, hidden, LANES), BF16),
            V((levels, nfield, ncols), BF16),
            DMA((8,)), DMA((2, 4)), DMA((2, 4)), DMA((2, 2)), DMA((2, 2)), DMA((2, 2)), DMA((2, 2)),
            DMA((2, 2)), DMA((2, 2)), DMA((2, 2)), DMA((2, 2)), DMA((2, 4)),
        ],
        compiler_params=pltpu.CompilerParams(
            collective_id=0, has_side_effects=True, vmem_limit_bytes=40 << 20
        ),
    )(
        fields.transpose(1, 0, 2),
        depart,
        fraction.transpose(1, 0, 2),
        w_first.reshape(-1, hidden),
        w_last.reshape(-1, hidden),
        w_middle,
        b_first[None, :],
        b_middle[None, :],
    )
    return result.transpose(1, 0, 2)


def solution(mesh):
    placed = (P(None, "lev", "band"), P("lev", "band"), P(None, "lev", "band"), P(), P(), P(), P(), P())
    return jax.shard_map(
        functools.partial(on_device, mesh.shape["band"], mesh.shape["lev"]),
        mesh=mesh,
        in_specs=placed,
        out_specs=P(None, "lev", "band"),
        check_vma=False,
    )
```

```python
import functools

import jax
import jax.numpy as jnp
from jax import lax
from jax.experimental import pallas as pl
from jax.experimental.pallas import tpu as pltpu
from jax.sharding import PartitionSpec as P

MESH = pl.DeviceIdType.MESH
F32, BF16 = jnp.float32, jnp.bfloat16
LANES = 128
ROW = 512

_PICK = lax.GatherDimensionNumbers(
    offset_dims=(),
    collapsed_slice_dims=(1,),
    start_index_map=(1,),
    operand_batching_dims=(0,),
    start_indices_batching_dims=(0,),
)


def lane_gather(x, lane):
    return lax.gather(
        x, lane[..., None], _PICK, (1, 1), mode=lax.GatherScatterMode.PROMISE_IN_BOUNDS
    )


def silu(v):
    return v / (1.0 + jnp.exp(-v))


def kernel(
    nband, nlev, fields, depart, fraction, w_first, w_last, w_middle, b_first, b_middle, out,
    ext, dep_v, frac_v, wf_v, wl_v, wm_v, bf_v, bm_v, p16, w00, w01, w10, w11,
    adv, w1t, w3, w2t, b1, b2, part, opp_tx, opp_rx, near_tx, near_rx, mid, out_v,
    load_sem, halo_send, halo_recv, opp_send, opp_recv, near_send, near_recv,
    mid_send, mid_recv, fwd_send, fwd_recv, store_sem,
):
    band, me = lax.axis_index("band"), lax.axis_index("lev")
    nrow = adv.shape[0]
    levels = nrow // 8
    core = lax.rem(band, 2)
    east, west = lax.rem(band + 1, nband), lax.rem(band + nband - 1, nband)
    up, down, far = lax.rem(me + 1, nlev), lax.rem(me + nlev - 1, nlev), lax.rem(me + 2, nlev)

    barrier = pltpu.get_barrier_semaphore()
    for peer in ({"band": east}, {"band": west}, {"lev": up}, {"lev": down}):
        pl.semaphore_signal(barrier, inc=1, device_id=peer, device_id_type=MESH)

    loads = [
        pltpu.make_async_copy(src, dst, load_sem.at[n])
        for n, (src, dst) in enumerate(
            (
                (depart, dep_v), (fraction, frac_v), (w_first, wf_v), (w_last, wl_v), (w_middle, wm_v),
                (b_first, bf_v), (b_middle, bm_v), (fields, ext.at[:, :, pl.ds(ROW, 2 * ROW)]),
            )
        )
    ]
    for load in loads:
        load.start()
    pl.semaphore_wait(barrier, 4)

    halos = []
    for i in range(4):
        for side, peer, src, dst in ((0, east, 7 - i, 3 - i), (1, west, i, 12 + i)):
            copy = pltpu.make_async_remote_copy(
                src_ref=fields.at[:, :, pl.ds(src * LANES, LANES)],
                dst_ref=ext.at[:, :, pl.ds(dst * LANES, LANES)],
                send_sem=halo_send.at[side, i],
                recv_sem=halo_recv.at[side, i],
                device_id={"band": peer},
                device_id_type=MESH,
            )
            copy.start()
            halos.append(copy)

    loads[0].wait()
    loads[1].wait()

    def prepare(i, carry):
        lane = lax.rem(lax.broadcasted_iota(jnp.int32, (8, 2 * ROW), 1), LANES) + ROW
        where, weights = [], []
        for j in range(2):
            level = 2 * i + j
            where.append(lane + jnp.broadcast_to(dep_v[pl.ds(level, 1), :], (8, 2 * ROW)))
            both = frac_v[level].astype(F32)
            a = jnp.broadcast_to(both[0:1], (8, 2 * ROW))
            b = jnp.broadcast_to(both[1:2], (8, 2 * ROW))
            weights.append(((1.0 - a) * (1.0 - b), a * (1.0 - b), (1.0 - a) * b, a * b))
        rows = pl.ds(pl.multiple_of(16 * i, 16), 16)
        p16[rows, :] = jnp.concatenate(where, axis=0).astype(jnp.int16)
        for ref, one, two in zip((w00, w01, w10, w11), *weights):
            ref[rows, :] = jnp.concatenate([one, two], axis=0)
        return carry

    lax.fori_loop(0, levels // 2, prepare, 0)

    for load in loads[2:7]:
        load.wait()
    total_rows = wf_v.shape[0]
    total_levels = total_rows // 8
    r = lax.broadcasted_iota(jnp.int32, (nrow, total_rows), 0)
    source = (r & 7) * total_levels + me * levels + (r >> 3)
    pick = jnp.where(lax.broadcasted_iota(jnp.int32, (nrow, total_rows), 1) == source, 1.0, 0.0).astype(BF16)
    w3[...] = jnp.dot(pick, wl_v[...], preferred_element_type=F32).astype(BF16)
    w1t[...] = jnp.dot(pick, wf_v[...], preferred_element_type=F32).T.astype(BF16)
    w2t[...] = wm_v[...].astype(F32).T.astype(BF16)
    b1[...] = jnp.broadcast_to(bf_v[...], (LANES, bf_v.shape[1])).T
    b2[...] = jnp.broadcast_to(bm_v[...], (LANES, bm_v.shape[1])).T
    loads[7].wait()

    def advect(block):
        base = pl.multiple_of(block * LANES, LANES)
        cols = pl.ds(base, LANES)

        for g in range(nrow // 16):
            rows = slice(16 * g, 16 * g + 16)
            p = p16[rows, cols]
            tiles = [
                ext[2 * g : 2 * g + 2, :, pl.ds(base + LANES * t, LANES)].reshape(16, LANES) for t in range(9)
            ]
            total = None
            for off, near, beyond in ((0, w00, w10), (1, w01, w11)):
                q = p + jnp.int16(off)
                lane = q & jnp.int16(LANES - 1)
                masks = [q >= jnp.int16(LANES * j) for j in range(1, 5)]
                got = [lane_gather(t, lane) for t in tiles]
                for start, weight in ((0, near), (4, beyond)):
                    value = got[start]
                    for j in range(4):
                        value = jnp.where(masks[j], got[start + j + 1], value)
                    term = weight[rows, cols] * value.astype(F32)
                    total = term if total is None else total + term
            adv[rows, cols] = total.astype(BF16)
        return cols

    def block_of(half, i):
        right = (1 - core) if half == 0 else core
        return right, right * (4 + i) + (1 - right) * (3 - i)

    def forward(half, i):
        right, block = block_of(half, i)
        tile = right * (12 + i) + (1 - right) * (3 - i)
        pltpu.make_async_remote_copy(
            src_ref=fields.at[:, :, pl.ds(0, LANES)],
            dst_ref=ext.at[:, :, pl.ds(pl.multiple_of(tile * LANES, LANES), LANES)],
            send_sem=halo_send.at[right, i],
            recv_sem=halo_recv.at[right, i],
            device_id={"band": east},
            device_id_type=MESH,
        ).wait_recv()
        cols = advect(block)
        part[half, i] = jnp.dot(w1t[...], adv[:, cols], preferred_element_type=F32)

    def remote(src, dst, send, recv, peer):
        return pltpu.make_async_remote_copy(
            src_ref=src, dst_ref=dst, send_sem=send, recv_sem=recv, device_id={"lev": peer}, device_id_type=MESH
        )

    hidden = w1t.shape[0]
    top, bottom = pl.ds(0, hidden // 2), pl.ds(hidden // 2, hidden // 2)
    sent = []

    def send_far(half):
        opp_tx[half] = part[half, far].astype(BF16)
        for way, rows, peer in ((0, top, up), (1, bottom, down)):
            copy = remote(
                opp_tx.at[half, rows], opp_rx.at[half, way], opp_send.at[half, way], opp_recv.at[half, way], peer
            )
            copy.start()
            sent.append(copy)

    def send_near(half):
        for way, rows, other, peer in ((0, top, bottom, up), (1, bottom, top, down)):
            remote(
                opp_tx.at[half, rows], opp_rx.at[half, way], opp_send.at[half, way], opp_recv.at[half, way], peer
            ).wait_recv()
            near_tx[half, way, rows] = (part[half, peer, rows] + opp_rx[half, way].astype(F32)).astype(BF16)
            near_tx[half, way, other] = part[half, peer, other].astype(BF16)
            copy = remote(
                near_tx.at[half, way], near_rx.at[half, way], near_send.at[half, way], near_recv.at[half, way], peer
            )
            copy.start()
            sent.append(copy)

    def finish(half):
        total = part[half, me] + b1[...]
        for way, peer in ((0, up), (1, down)):
            remote(
                near_tx.at[half, way], near_rx.at[half, way], near_send.at[half, way], near_recv.at[half, way], peer
            ).wait_recv()
            total = total + near_rx[half, way].astype(F32)
        first = silu(total).astype(BF16)
        second = jnp.dot(w2t[...], first, preferred_element_type=F32) + b2[...]
        mid[half, me] = silu(second).astype(BF16)
        for way, peer in ((0, up), (1, down)):
            copy = remote(
                mid.at[half, me], mid.at[half, me], mid_send.at[half, way], mid_recv.at[half, way], peer
            )
            copy.start()
            sent.append(copy)

    def pass_on(half):
        for way, rows, owner, peer in ((0, top, down, up), (1, bottom, up, down)):
            remote(
                mid.at[half, owner], mid.at[half, owner], mid_send.at[half, way], mid_recv.at[half, way], peer
            ).wait_recv()
            copy = remote(
                mid.at[half, owner, rows], mid.at[half, owner, rows],
                fwd_send.at[half, way], fwd_recv.at[half, way], peer,
            )
            copy.start()
            sent.append(copy)

    stores = []

    def last(half, i):
        _, block = block_of(half, i)
        cols = pl.ds(pl.multiple_of(block * LANES, LANES), LANES)
        tendency = jnp.dot(w3[...], mid[half, i], preferred_element_type=F32)
        updated = (adv[:, cols].astype(F32) + tendency).astype(BF16)
        out_v[:, :, cols] = updated.reshape(levels, 8, LANES)
        store = pltpu.make_async_copy(out_v.at[:, :, cols], out.at[:, :, cols], store_sem.at[half, i])
        store.start()
        stores.append(store)

    def finale(half):
        last(half, me)
        last(half, up)
        last(half, down)
        for way, rows, peer in ((0, top, up), (1, bottom, down)):
            remote(
                mid.at[half, far, rows], mid.at[half, far, rows],
                fwd_send.at[half, way], fwd_recv.at[half, way], peer,
            ).wait_recv()
        last(half, far)

    for i in range(4):
        forward(0, i)
    send_far(0)
    forward(1, 0)
    send_near(0)
    forward(1, 1)
    forward(1, 2)
    finish(0)
    forward(1, 3)
    send_far(1)
    pass_on(0)
    send_near(1)
    finale(0)
    finish(1)
    pass_on(1)
    finale(1)

    for copy in halos + sent:
        copy.wait_send()
    for store in stores:
        store.wait()


def on_device(nband, nlev, fields, depart, fraction, w_first, b_first, w_middle, b_middle, w_last):
    nfield, levels, ncols = fields.shape
    nrow, hidden = nfield * levels, w_middle.shape[0]
    V, DMA = pltpu.VMEM, pltpu.SemaphoreType.DMA
    table = V((nrow, ncols), F32)
    whole = V((nfield * w_first.shape[1], hidden), BF16)
    result = pl.pallas_call(
        functools.partial(kernel, nband, nlev),
        out_shape=jax.ShapeDtypeStruct((levels, nfield, ncols), BF16),
        in_specs=[pl.BlockSpec(memory_space=pltpu.HBM)] * 8,
        out_specs=pl.BlockSpec(memory_space=pltpu.HBM),
        scratch_shapes=[
            V((levels, nfield, 2 * ncols), BF16),
            V((levels, ncols), jnp.int32),
            V((levels, 2, ncols), BF16),
            whole,
            whole,
            V((hidden, hidden), BF16),
            V((1, hidden), F32),
            V((1, hidden), F32),
            V((nrow, ncols), jnp.int16),
            table, table, table, table,
            V((nrow, ncols), BF16),
            V((hidden, nrow), BF16),
            V((nrow, hidden), BF16),
            V((hidden, hidden), BF16),
            V((hidden, LANES), F32),
            V((hidden, LANES), F32),
            V((2, 4, hidden, LANES), F32),
            V((2, hidden, LANES), BF16),
            V((2, 2, hidden // 2, LANES), BF16),
            V((2, 2, hidden, LANES), BF16),
            V((2, 2, hidden, LANES), BF16),
            V((2, 4, hidden, LANES), BF16),
            V((levels, nfield, ncols), BF16),
            DMA((8,)), DMA((2, 4)), DMA((2, 4)), DMA((2, 2)), DMA((2, 2)), DMA((2, 2)), DMA((2, 2)),
            DMA((2, 2)), DMA((2, 2)), DMA((2, 2)), DMA((2, 2)), DMA((2, 4)),
        ],
        compiler_params=pltpu.CompilerParams(
            collective_id=0, has_side_effects=True, vmem_limit_bytes=60 << 20
        ),
    )(
        fields.transpose(1, 0, 2),
        depart,
        fraction.transpose(1, 0, 2),
        w_first.reshape(-1, hidden),
        w_last.reshape(-1, hidden),
        w_middle,
        b_first[None, :],
        b_middle[None, :],
    )
    return result.transpose(1, 0, 2)


def solution(mesh):
    placed = (P(None, "lev", "band"), P("lev", "band"), P(None, "lev", "band"), P(), P(), P(), P(), P())
    return jax.shard_map(
        functools.partial(on_device, mesh.shape["band"], mesh.shape["lev"]),
        mesh=mesh,
        in_specs=placed,
        out_specs=P(None, "lev", "band"),
        check_vma=False,
    )
```

```python
import functools

import jax
import jax.numpy as jnp
from jax import lax
from jax.experimental import pallas as pl
from jax.experimental.pallas import tpu as pltpu
from jax.sharding import PartitionSpec as P

MESH = pl.DeviceIdType.MESH
F32, BF16 = jnp.float32, jnp.bfloat16
LANES = 128
ROW = 512

_PICK = lax.GatherDimensionNumbers(
    offset_dims=(),
    collapsed_slice_dims=(1,),
    start_index_map=(1,),
    operand_batching_dims=(0,),
    start_indices_batching_dims=(0,),
)


def lane_gather(x, lane):
    return lax.gather(
        x, lane[..., None], _PICK, (1, 1), mode=lax.GatherScatterMode.PROMISE_IN_BOUNDS
    )


def silu(v):
    return v / (1.0 + jnp.exp(-v))


def kernel(
    nband, nlev, fields, depart, fraction, w_first, w_last, w_middle, b_first, b_middle, out,
    ext, dep_v, frac_v, wf_v, wl_v, wm_v, bf_v, bm_v, p16, w00, w01, w10, w11,
    adv, w1t, w3, w2t, b1, b2, part, part_tx, part_rx, mid, out_v,
    load_sem, halo_send, halo_recv, part_send, part_recv, mid_send, mid_recv, store_sem,
):
    band, me = lax.axis_index("band"), lax.axis_index("lev")
    nrow = adv.shape[0]
    levels = nrow // 8
    core = lax.rem(band, 2)
    east, west = lax.rem(band + 1, nband), lax.rem(band + nband - 1, nband)
    up, down, far = lax.rem(me + 1, nlev), lax.rem(me + nlev - 1, nlev), lax.rem(me + 2, nlev)

    barrier = pltpu.get_barrier_semaphore()
    for peer in ({"band": east}, {"band": west}, {"lev": up}, {"lev": down}, {"lev": far}):
        pl.semaphore_signal(barrier, inc=1, device_id=peer, device_id_type=MESH)

    loads = [
        pltpu.make_async_copy(src, dst, load_sem.at[n])
        for n, (src, dst) in enumerate(
            (
                (depart, dep_v), (fraction, frac_v), (fields, ext.at[:, :, pl.ds(ROW, 2 * ROW)]),
                (w_first, wf_v), (w_last, wl_v), (w_middle, wm_v), (b_first, bf_v), (b_middle, bm_v),
            )
        )
    ]
    for load in loads:
        load.start()
    pl.semaphore_wait(barrier, 5)

    halos = []
    for i in range(4):
        for side, peer, src, dst in ((0, east, 7 - i, 3 - i), (1, west, i, 12 + i)):
            copy = pltpu.make_async_remote_copy(
                src_ref=fields.at[:, :, pl.ds(src * LANES, LANES)],
                dst_ref=ext.at[:, :, pl.ds(dst * LANES, LANES)],
                send_sem=halo_send.at[side, i],
                recv_sem=halo_recv.at[side, i],
                device_id={"band": peer},
                device_id_type=MESH,
            )
            copy.start()
            halos.append(copy)

    loads[0].wait()
    loads[1].wait()

    def prepare(i, carry):
        lane = lax.rem(lax.broadcasted_iota(jnp.int32, (8, 2 * ROW), 1), LANES) + ROW
        where, weights = [], []
        for j in range(2):
            level = 2 * i + j
            where.append(lane + jnp.broadcast_to(dep_v[pl.ds(level, 1), :], (8, 2 * ROW)))
            both = frac_v[level].astype(F32)
            a = jnp.broadcast_to(both[0:1], (8, 2 * ROW))
            b = jnp.broadcast_to(both[1:2], (8, 2 * ROW))
            weights.append(((1.0 - a) * (1.0 - b), a * (1.0 - b), (1.0 - a) * b, a * b))
        rows = pl.ds(pl.multiple_of(16 * i, 16), 16)
        p16[rows, :] = jnp.concatenate(where, axis=0).astype(jnp.int16)
        for ref, one, two in zip((w00, w01, w10, w11), *weights):
            ref[rows, :] = jnp.concatenate([one, two], axis=0)
        return carry

    lax.fori_loop(0, levels // 2, prepare, 0)

    for load in loads[3:]:
        load.wait()
    total_rows = wf_v.shape[0]
    total_levels = total_rows // 8
    r = lax.broadcasted_iota(jnp.int32, (nrow, total_rows), 0)
    source = (r & 7) * total_levels + me * levels + (r >> 3)
    pick = jnp.where(lax.broadcasted_iota(jnp.int32, (nrow, total_rows), 1) == source, 1.0, 0.0).astype(BF16)
    w3[...] = jnp.dot(pick, wl_v[...], preferred_element_type=F32).astype(BF16)
    w1t[...] = jnp.dot(pick, wf_v[...], preferred_element_type=F32).T.astype(BF16)
    w2t[...] = wm_v[...].astype(F32).T.astype(BF16)
    b1[...] = jnp.broadcast_to(bf_v[...], (LANES, bf_v.shape[1])).T
    b2[...] = jnp.broadcast_to(bm_v[...], (LANES, bm_v.shape[1])).T
    loads[2].wait()

    def advect(block):
        base = pl.multiple_of(block * LANES, LANES)
        cols = pl.ds(base, LANES)

        for g in range(nrow // 16):
            rows = slice(16 * g, 16 * g + 16)
            p = p16[rows, cols]
            tiles = [
                ext[2 * g : 2 * g + 2, :, pl.ds(base + LANES * t, LANES)].reshape(16, LANES) for t in range(9)
            ]
            total = None
            for off, near, beyond in ((0, w00, w10), (1, w01, w11)):
                q = p + jnp.int16(off)
                lane = q & jnp.int16(LANES - 1)
                masks = [q >= jnp.int16(LANES * j) for j in range(1, 5)]
                got = [lane_gather(t, lane) for t in tiles]
                for start, weight in ((0, near), (4, beyond)):
                    value = got[start]
                    for j in range(4):
                        value = jnp.where(masks[j], got[start + j + 1], value)
                    term = weight[rows, cols] * value.astype(F32)
                    total = term if total is None else total + term
            adv[rows, cols] = total.astype(BF16)
        return cols

    def block_of(half, i):
        right = (1 - core) if half == 0 else core
        return right, right * (4 + i) + (1 - right) * (3 - i)

    def forward(half, i):
        right, block = block_of(half, i)
        tile = right * (12 + i) + (1 - right) * (3 - i)
        pltpu.make_async_remote_copy(
            src_ref=fields.at[:, :, pl.ds(0, LANES)],
            dst_ref=ext.at[:, :, pl.ds(pl.multiple_of(tile * LANES, LANES), LANES)],
            send_sem=halo_send.at[right, i],
            recv_sem=halo_recv.at[right, i],
            device_id={"band": east},
            device_id_type=MESH,
        ).wait_recv()
        cols = advect(block)
        part[half, i] = jnp.dot(w1t[...], adv[:, cols], preferred_element_type=F32)

    def remote(src, dst, send, recv, peer):
        return pltpu.make_async_remote_copy(
            src_ref=src, dst_ref=dst, send_sem=send, recv_sem=recv, device_id={"lev": peer}, device_id_type=MESH
        )

    def partial_copy(half, i):
        slot = lax.rem(me - i + nlev, nlev)
        return remote(
            part_tx.at[half, i], part_rx.at[half, slot], part_send.at[half, i], part_recv.at[half, slot], i
        )

    def send_partial(half, i):
        @pl.when(me != i)
        def _():
            part_tx[half, i] = part[half, i].astype(BF16)
            partial_copy(half, i).start()

    def middle_copy(half, owner, hop):
        return remote(
            mid.at[half, owner], mid.at[half, owner], mid_send.at[half, hop], mid_recv.at[half, owner],
            lax.rem(owner + hop, nlev),
        )

    def finish(half):
        total = part[half, me] + b1[...]
        for slot in range(1, nlev):
            remote(
                part_tx.at[half, 0], part_rx.at[half, slot], part_send.at[half, 0], part_recv.at[half, slot], far
            ).wait_recv()
            total = total + part_rx[half, slot].astype(F32)
        first = silu(total).astype(BF16)
        second = jnp.dot(w2t[...], first, preferred_element_type=F32) + b2[...]
        mid[half, me] = silu(second).astype(BF16)
        for hop in (2, 1, 3):
            middle_copy(half, me, hop).start()

    stores = []

    def last(half, i):
        _, block = block_of(half, i)
        cols = pl.ds(pl.multiple_of(block * LANES, LANES), LANES)
        tendency = jnp.dot(w3[...], mid[half, i], preferred_element_type=F32)
        updated = (adv[:, cols].astype(F32) + tendency).astype(BF16)
        out_v[:, :, cols] = updated.reshape(levels, 8, LANES)
        store = pltpu.make_async_copy(out_v.at[:, :, cols], out.at[:, :, cols], store_sem.at[half, i])
        store.start()
        stores.append(store)

    def finale(half):
        last(half, me)
        for hop in (1, 3, 2):
            owner = lax.rem(me + hop, nlev)
            middle_copy(half, owner, nlev - hop).wait_recv()
            last(half, owner)

    for half in range(2):
        for i in range(nlev):
            forward(half, i)
            send_partial(half, i)
    finish(0)
    finish(1)
    finale(0)
    finale(1)

    for half in range(2):
        for i in range(nlev):
            @pl.when(me != i)
            def _():
                partial_copy(half, i).wait_send()
        for hop in range(1, nlev):
            middle_copy(half, me, hop).wait_send()
    for copy in halos:
        copy.wait_send()
    for store in stores:
        store.wait()


def on_device(nband, nlev, fields, depart, fraction, w_first, b_first, w_middle, b_middle, w_last):
    nfield, levels, ncols = fields.shape
    nrow, hidden = nfield * levels, w_middle.shape[0]
    V, DMA = pltpu.VMEM, pltpu.SemaphoreType.DMA
    table = V((nrow, ncols), F32)
    whole = V((nfield * w_first.shape[1], hidden), BF16)
    result = pl.pallas_call(
        functools.partial(kernel, nband, nlev),
        out_shape=jax.ShapeDtypeStruct((levels, nfield, ncols), BF16),
        in_specs=[pl.BlockSpec(memory_space=pltpu.HBM)] * 8,
        out_specs=pl.BlockSpec(memory_space=pltpu.HBM),
        scratch_shapes=[
            V((levels, nfield, 2 * ncols), BF16),
            V((levels, ncols), jnp.int32),
            V((levels, 2, ncols), BF16),
            whole,
            whole,
            V((hidden, hidden), BF16),
            V((1, hidden), F32),
            V((1, hidden), F32),
            V((nrow, ncols), jnp.int16),
            table, table, table, table,
            V((nrow, ncols), BF16),
            V((hidden, nrow), BF16),
            V((nrow, hidden), BF16),
            V((hidden, hidden), BF16),
            V((hidden, LANES), F32),
            V((hidden, LANES), F32),
            V((2, 4, hidden, LANES), F32),
            V((2, 4, hidden, LANES), BF16),
            V((2, 4, hidden, LANES), BF16),
            V((2, 4, hidden, LANES), BF16),
            V((levels, nfield, ncols), BF16),
            DMA((8,)), DMA((2, 4)), DMA((2, 4)), DMA((2, 4)), DMA((2, 4)), DMA((2, 4)), DMA((2, 4)), DMA((2, 4)),
        ],
        compiler_params=pltpu.CompilerParams(
            collective_id=0, has_side_effects=True, vmem_limit_bytes=60 << 20
        ),
    )(
        fields.transpose(1, 0, 2),
        depart,
        fraction.transpose(1, 0, 2),
        w_first.reshape(-1, hidden),
        w_last.reshape(-1, hidden),
        w_middle,
        b_first[None, :],
        b_middle[None, :],
    )
    return result.transpose(1, 0, 2)


def solution(mesh):
    placed = (P(None, "lev", "band"), P("lev", "band"), P(None, "lev", "band"), P(), P(), P(), P(), P())
    return jax.shard_map(
        functools.partial(on_device, mesh.shape["band"], mesh.shape["lev"]),
        mesh=mesh,
        in_specs=placed,
        out_specs=P(None, "lev", "band"),
        check_vma=False,
    )
```

```python
import functools

import jax
import jax.numpy as jnp
from jax import lax
from jax.experimental import pallas as pl
from jax.experimental.pallas import tpu as pltpu
from jax.sharding import PartitionSpec as P

MESH = pl.DeviceIdType.MESH
F32, BF16 = jnp.float32, jnp.bfloat16
LANES = 128
WINDOW = 48
ROW = 512

_PICK = lax.GatherDimensionNumbers(
    offset_dims=(),
    collapsed_slice_dims=(1,),
    start_index_map=(1,),
    operand_batching_dims=(0,),
    start_indices_batching_dims=(0,),
)


def lane_gather(x, lane):
    return lax.gather(
        x, lane[..., None], _PICK, (1, 1), mode=lax.GatherScatterMode.PROMISE_IN_BOUNDS
    )


def silu(v):
    return v / (1.0 + jnp.exp(-v))


def kernel(
    nband, nlev, fields, depart, fraction, w_first, w_last, w_middle, b_first, b_middle, out,
    ext, dep_v, frac_v, wf_v, wl_v, wm_v, bf_v, bm_v, p16, w00, w01, w10, w11,
    adv, w1t, w3, w2t, b1, b2, part, part_tx, part_rx, mid,
    load_sem, halo_send, halo_recv, part_send, part_recv, mid_send, mid_recv,
    west_in, peers_in, lev_in,
):
    band, me = lax.axis_index("band"), lax.axis_index("lev")
    nrow = adv.shape[0]
    levels = nrow // 8
    core = lax.rem(band, 2)
    east, west = lax.rem(band + 1, nband), lax.rem(band + nband - 1, nband)
    up, down, far = lax.rem(me + 1, nlev), lax.rem(me + nlev - 1, nlev), lax.rem(me + 2, nlev)

    is_first = core == 0
    barrier = pltpu.get_barrier_semaphore()
    others = [lax.rem(me + hop, nlev) for hop in range(1, nlev)]

    def tell(sem, peer):
        pl.semaphore_signal(sem, inc=1, device_id=peer, device_id_type=MESH)

    @pl.when(is_first)
    def _():
        tell(barrier, {"band": west})
        tell(barrier, {"band": east})
        for peer in others:
            tell(barrier, {"lev": peer})

    @pl.when(jnp.logical_not(is_first))
    def _():
        tell(barrier, {"band": west})

    pairs_of_refs = [(depart, dep_v), (fraction, frac_v), (fields, ext.at[:, :, pl.ds(ROW, 2 * ROW)])]
    for src, dst in ((w_first, wf_v), (w_last, wl_v)):
        for f in range(8):
            start = pl.multiple_of((f * nlev * levels + me * levels) // 16 * 16, 16)
            pairs_of_refs.append((src.at[pl.ds(start, WINDOW)], dst.at[pl.ds(f * WINDOW, WINDOW)]))
    pairs_of_refs += [(w_middle, wm_v), (b_first, bf_v), (b_middle, bm_v)]
    loads = [
        pltpu.make_async_copy(src, dst, load_sem.at[n]) for n, (src, dst) in enumerate(pairs_of_refs)
    ]
    for load in loads:
        load.start()

    @pl.when(is_first)
    def _():
        pl.semaphore_wait(barrier, nlev)
        for peer in others:
            tell(peers_in, {"lev": peer})

    @pl.when(jnp.logical_not(is_first))
    def _():
        pl.semaphore_wait(barrier, 2)
        tell(west_in, {"band": east})


    def halo_copy(right, i, tiles=1):
        src = right * (8 - tiles - i) + (1 - right) * i
        dst = right * (4 - tiles - i) + (1 - right) * (12 + i)
        return pltpu.make_async_remote_copy(
            src_ref=fields.at[:, :, pl.ds(pl.multiple_of(src * LANES, LANES), tiles * LANES)],
            dst_ref=ext.at[:, :, pl.ds(pl.multiple_of(dst * LANES, LANES), tiles * LANES)],
            send_sem=halo_send.at[tiles // 4, i],
            recv_sem=halo_recv.at[tiles // 4, i],
            device_id={"band": right * east + (1 - right) * west},
            device_id_type=MESH,
        )

    def prepare(i, carry):
        lane = lax.rem(lax.broadcasted_iota(jnp.int32, (8, 2 * ROW), 1), LANES) + ROW
        where, weights = [], []
        for j in range(2):
            level = 2 * i + j
            where.append(lane + jnp.broadcast_to(dep_v[pl.ds(level, 1), :], (8, 2 * ROW)))
            both = frac_v[level].astype(F32)
            a = jnp.broadcast_to(both[0:1], (8, 2 * ROW))
            b = jnp.broadcast_to(both[1:2], (8, 2 * ROW))
            weights.append(((1.0 - a) * (1.0 - b), a * (1.0 - b), (1.0 - a) * b, a * b))
        rows = pl.ds(pl.multiple_of(16 * i, 16), 16)
        p16[rows, :] = jnp.concatenate(where, axis=0).astype(jnp.int16)
        for ref, one, two in zip((w00, w01, w10, w11), *weights):
            ref[rows, :] = jnp.concatenate([one, two], axis=0)
        return carry

    def send_slow():
        @pl.when(is_first)
        def _():
            pl.semaphore_wait(west_in, 1)

        for i in range(4):
            halo_copy(core, i).start()

    ahead = lax.rem(band, 16) == 0
    halo_copy(1 - core, 0, 4).start()
    pl.when(jnp.logical_not(ahead))(send_slow)
    loads[0].wait()
    loads[1].wait()
    lax.fori_loop(0, levels // 2, prepare, 0)

    for load in loads[3:]:
        load.wait()
    r = lax.broadcasted_iota(jnp.int32, (nrow, 8 * WINDOW), 0)
    field = r & 7
    source = field * WINDOW + (field & 1) * 8 + me * 2 + (r >> 3)
    pick = jnp.where(lax.broadcasted_iota(jnp.int32, (nrow, 8 * WINDOW), 1) == source, 1.0, 0.0).astype(BF16)
    w1t[...] = jnp.dot(pick, wf_v[...], preferred_element_type=F32).T.astype(BF16)
    w3[...] = jnp.dot(pick, wl_v[...], preferred_element_type=F32).astype(BF16)
    w2t[...] = wm_v[...].astype(F32).T.astype(BF16)
    b1[...] = jnp.broadcast_to(bf_v[...], (LANES, bf_v.shape[1])).T
    b2[...] = jnp.broadcast_to(bm_v[...], (LANES, bm_v.shape[1])).T
    loads[2].wait()

    def advect(block):
        base = pl.multiple_of(block * LANES, LANES)
        cols = pl.ds(base, LANES)

        for g in range(nrow // 16):
            rows = slice(16 * g, 16 * g + 16)
            p = p16[rows, cols]
            tiles = [
                ext[2 * g : 2 * g + 2, :, pl.ds(base + LANES * t, LANES)].reshape(16, LANES) for t in range(9)
            ]
            total = None
            for off, near, beyond in ((0, w00, w10), (1, w01, w11)):
                q = p + jnp.int16(off)
                lane = q & jnp.int16(LANES - 1)
                masks = [q >= jnp.int16(LANES * j) for j in range(1, 5)]
                got = [lane_gather(t, lane) for t in tiles]
                for start, weight in ((0, near), (4, beyond)):
                    value = got[start]
                    for j in range(4):
                        value = jnp.where(masks[j], got[start + j + 1], value)
                    term = weight[rows, cols] * value.astype(F32)
                    total = term if total is None else total + term
            adv[rows, cols] = total.astype(BF16)
        return cols

    def block_of(half, i):
        right = (1 - core) if half == 0 else core
        return right, right * (4 + i) + (1 - right) * (3 - i)

    def forward(half, i):
        right, block = block_of(half, i)
        if half == 1:
            halo_copy(1 - right, i).wait_recv()
        elif i == 0:
            halo_copy(1 - right, 0, 4).wait_recv()
        cols = advect(block)
        part[half, i] = jnp.dot(w1t[...], adv[:, cols], preferred_element_type=F32)

    def remote(src, dst, send, recv, peer):
        return pltpu.make_async_remote_copy(
            src_ref=src, dst_ref=dst, send_sem=send, recv_sem=recv, device_id={"lev": peer}, device_id_type=MESH
        )

    def partial_copy(half, i):
        slot = lax.rem(me - i + nlev, nlev)
        return remote(
            part_tx.at[half, i], part_rx.at[half, slot], part_send.at[half, i], part_recv.at[half, slot], i
        )

    def send_partial(half, i):
        @pl.when(me != i)
        def _():
            part_tx[half, i] = part[half, i].astype(BF16)
            partial_copy(half, i).start()

    def middle_copy(half, owner, hop):
        return remote(
            mid.at[half, owner], mid.at[half, owner], mid_send.at[half, hop], mid_recv.at[half, owner],
            lax.rem(owner + hop, nlev),
        )

    def finish(half):
        total = part[half, me] + b1[...]
        for slot in range(1, nlev):
            remote(
                part_tx.at[half, 0], part_rx.at[half, slot], part_send.at[half, 0], part_recv.at[half, slot], far
            ).wait_recv()
            total = total + part_rx[half, slot].astype(F32)
        first = silu(total).astype(BF16)
        second = jnp.dot(w2t[...], first, preferred_element_type=F32) + b2[...]
        mid[half, me] = silu(second).astype(BF16)
        for hop in (2, 1, 3):
            middle_copy(half, me, hop).start()

    def last(half, i):
        _, block = block_of(half, i)
        cols = pl.ds(pl.multiple_of(block * LANES, LANES), LANES)
        tendency = jnp.dot(w3[...], mid[half, i], preferred_element_type=F32)
        updated = (adv[:, cols].astype(F32) + tendency).astype(BF16)
        out[:, :, cols] = updated.reshape(levels, 8, LANES)

    def finale(half):
        last(half, me)
        for hop in (1, 3, 2):
            owner = lax.rem(me + hop, nlev)
            middle_copy(half, owner, nlev - hop).wait_recv()
            last(half, owner)

    @pl.when(is_first)
    def _():
        pl.semaphore_wait(peers_in, nlev - 1)
        tell(lev_in, {"band": east})

    for i in range(nlev):
        forward(0, i)
        if i == 0:
            @pl.when(jnp.logical_not(is_first))
            def _():
                pl.semaphore_wait(lev_in, 1)

        send_partial(0, i)
    pl.when(ahead)(send_slow)
    for i in range(nlev):
        forward(1, i)
        send_partial(1, i)
    finish(0)
    finish(1)
    finale(0)
    finale(1)

    for half in range(2):
        for i in range(nlev):
            @pl.when(me != i)
            def _():
                partial_copy(half, i).wait_send()
        for hop in range(1, nlev):
            middle_copy(half, me, hop).wait_send()
    halo_copy(1 - core, 0, 4).wait_send()
    for i in range(4):
        halo_copy(core, i).wait_send()


def on_device(nband, nlev, fields, depart, fraction, w_first, b_first, w_middle, b_middle, w_last):
    nfield, levels, ncols = fields.shape
    nrow, hidden = nfield * levels, w_middle.shape[0]
    V, DMA = pltpu.VMEM, pltpu.SemaphoreType.DMA
    table = V((nrow, ncols), F32)
    window = V((nfield * WINDOW, hidden), BF16)
    operands = (
        fields.transpose(1, 0, 2),
        depart,
        fraction.transpose(1, 0, 2),
        w_first.reshape(-1, hidden),
        w_last.reshape(-1, hidden),
        w_middle,
        b_first[None, :],
        b_middle[None, :],
    )
    result = pl.pallas_call(
        functools.partial(kernel, nband, nlev),
        out_shape=jax.ShapeDtypeStruct((levels, nfield, ncols), BF16),
        in_specs=[pl.BlockSpec(memory_space=pltpu.HBM)] * 8,
        out_specs=pl.BlockSpec(memory_space=pltpu.VMEM),
        scratch_shapes=[
            V((levels, nfield, 2 * ncols), BF16),
            V((levels, ncols), jnp.int32),
            V((levels, 2, ncols), BF16),
            window,
            window,
            V((hidden, hidden), BF16),
            V((1, hidden), F32),
            V((1, hidden), F32),
            V((nrow, ncols), jnp.int16),
            table, table, table, table,
            V((nrow, ncols), BF16),
            V((hidden, nrow), BF16),
            V((nrow, hidden), BF16),
            V((hidden, hidden), BF16),
            V((hidden, LANES), F32),
            V((hidden, LANES), F32),
            V((2, 4, hidden, LANES), F32),
            V((2, 4, hidden, LANES), BF16),
            V((2, 4, hidden, LANES), BF16),
            V((2, 4, hidden, LANES), BF16),
            DMA((22,)), DMA((2, 4)), DMA((2, 4)), DMA((2, 4)), DMA((2, 4)), DMA((2, 4)), DMA((2, 4)),
            pltpu.SemaphoreType.REGULAR, pltpu.SemaphoreType.REGULAR, pltpu.SemaphoreType.REGULAR,
        ],
        compiler_params=pltpu.CompilerParams(
            collective_id=0, has_side_effects=True, vmem_limit_bytes=40 << 20
        ),
    )(
        *(pltpu.with_memory_space_constraint(x, pltpu.HBM) for x in operands)
    )
    return result.transpose(1, 0, 2)


def solution(mesh):
    placed = (P(None, "lev", "band"), P("lev", "band"), P(None, "lev", "band"), P(), P(), P(), P(), P())
    return jax.shard_map(
        functools.partial(on_device, mesh.shape["band"], mesh.shape["lev"]),
        mesh=mesh,
        in_specs=placed,
        out_specs=P(None, "lev", "band"),
        check_vma=False,
    )
```

```python
import functools

import jax
import jax.numpy as jnp
from jax import lax
from jax.experimental import pallas as pl
from jax.experimental.pallas import tpu as pltpu
from jax.sharding import PartitionSpec as P

MESH = pl.DeviceIdType.MESH
F32, BF16 = jnp.float32, jnp.bfloat16
LANES = 128
WINDOW = 48
QUARTER = 64
ROW = 512

_PICK = lax.GatherDimensionNumbers(
    offset_dims=(),
    collapsed_slice_dims=(1,),
    start_index_map=(1,),
    operand_batching_dims=(0,),
    start_indices_batching_dims=(0,),
)


def lane_gather(x, lane):
    return lax.gather(
        x, lane[..., None], _PICK, (1, 1), mode=lax.GatherScatterMode.PROMISE_IN_BOUNDS
    )


def silu(v):
    return v / (1.0 + jnp.exp(-v))


def kernel(
    nband, nlev, fields, depart, fraction, w_first, w_last, w_middle, b_first, b_middle, out,
    ext, dep_v, frac_v, wf_v, wl_v, wm_v, bf_v, bm_v, p16, w00, w01, w10, w11,
    adv, w1, w3, part, part_tx, part_rx, mid,
    load_sem, halo_send, halo_recv, part_send, part_recv, mid_send, mid_recv,
    west_in, peers_in, lev_in,
):
    band, me = lax.axis_index("band"), lax.axis_index("lev")
    nrow = adv.shape[0]
    levels = nrow // 8
    core = lax.rem(band, 2)
    east, west = lax.rem(band + 1, nband), lax.rem(band + nband - 1, nband)

    is_first = core == 0
    barrier = pltpu.get_barrier_semaphore()
    others = [lax.rem(me + hop, nlev) for hop in range(1, nlev)]

    def tell(sem, peer):
        pl.semaphore_signal(sem, inc=1, device_id=peer, device_id_type=MESH)

    @pl.when(is_first)
    def _():
        tell(barrier, {"band": west})
        tell(barrier, {"band": east})
        for peer in others:
            tell(barrier, {"lev": peer})

    @pl.when(jnp.logical_not(is_first))
    def _():
        tell(barrier, {"band": west})

    pairs_of_refs = [(depart, dep_v), (fraction, frac_v), (fields, ext.at[:, :, pl.ds(ROW, 2 * ROW)])]
    for src, dst in ((w_first, wf_v), (w_last, wl_v)):
        for f in range(8):
            start = pl.multiple_of((f * nlev * levels + me * levels) // 16 * 16, 16)
            pairs_of_refs.append((src.at[pl.ds(start, WINDOW)], dst.at[pl.ds(f * WINDOW, WINDOW)]))
    pairs_of_refs += [(w_middle, wm_v), (b_first, bf_v), (b_middle, bm_v)]
    loads = [
        pltpu.make_async_copy(src, dst, load_sem.at[n]) for n, (src, dst) in enumerate(pairs_of_refs)
    ]
    for load in loads:
        load.start()

    @pl.when(is_first)
    def _():
        pl.semaphore_wait(barrier, nlev)
        for peer in others:
            tell(peers_in, {"lev": peer})

    @pl.when(jnp.logical_not(is_first))
    def _():
        pl.semaphore_wait(barrier, 2)
        tell(west_in, {"band": east})


    def halo_copy(right, i, tiles=1):
        src = right * (8 - tiles - i) + (1 - right) * i
        dst = right * (4 - tiles - i) + (1 - right) * (12 + i)
        return pltpu.make_async_remote_copy(
            src_ref=fields.at[:, :, pl.ds(pl.multiple_of(src * LANES, LANES), tiles * LANES)],
            dst_ref=ext.at[:, :, pl.ds(pl.multiple_of(dst * LANES, LANES), tiles * LANES)],
            send_sem=halo_send.at[tiles // 4, i],
            recv_sem=halo_recv.at[tiles // 4, i],
            device_id={"band": right * east + (1 - right) * west},
            device_id_type=MESH,
        )

    def prepare(i, carry):
        lane = lax.rem(lax.broadcasted_iota(jnp.int32, (8, 2 * ROW), 1), LANES) + ROW
        where, weights = [], []
        for j in range(2):
            level = 2 * i + j
            where.append(lane + jnp.broadcast_to(dep_v[pl.ds(level, 1), :], (8, 2 * ROW)))
            both = frac_v[level].astype(F32)
            a = jnp.broadcast_to(both[0:1], (8, 2 * ROW))
            b = jnp.broadcast_to(both[1:2], (8, 2 * ROW))
            weights.append(((1.0 - a) * (1.0 - b), a * (1.0 - b), (1.0 - a) * b, a * b))
        rows = pl.ds(pl.multiple_of(16 * i, 16), 16)
        p16[rows, :] = jnp.concatenate(where, axis=0).astype(jnp.int16)
        for ref, one, two in zip((w00, w01, w10, w11), *weights):
            ref[rows, :] = jnp.concatenate([one, two], axis=0)
        return carry

    def send_slow():
        @pl.when(is_first)
        def _():
            pl.semaphore_wait(west_in, 1)

        for i in range(4):
            halo_copy(core, i).start()

    ahead = lax.rem(band, 16) == 0
    halo_copy(1 - core, 0, 4).start()
    pl.when(jnp.logical_not(ahead))(send_slow)
    loads[0].wait()
    loads[1].wait()
    lax.fori_loop(0, levels // 2, prepare, 0)

    for load in loads[3:]:
        load.wait()
    r = lax.broadcasted_iota(jnp.int32, (nrow, 8 * WINDOW), 0)
    field = r & 7
    source = field * WINDOW + (field & 1) * 8 + me * 2 + (r >> 3)
    pick = jnp.where(lax.broadcasted_iota(jnp.int32, (nrow, 8 * WINDOW), 1) == source, 1.0, 0.0).astype(BF16)
    w1[...] = jnp.dot(pick, wf_v[...], preferred_element_type=F32).astype(BF16)
    w3[...] = jnp.dot(pick, wl_v[...], preferred_element_type=F32).astype(BF16)
    loads[2].wait()

    def advect(block):
        base = pl.multiple_of(block * LANES, LANES)
        cols = pl.ds(base, LANES)

        for g in range(nrow // 16):
            rows = slice(16 * g, 16 * g + 16)
            p = p16[rows, cols]
            tiles = [
                ext[2 * g : 2 * g + 2, :, pl.ds(base + LANES * t, LANES)].reshape(16, LANES) for t in range(9)
            ]
            total = None
            for off, near, beyond in ((0, w00, w10), (1, w01, w11)):
                q = p + jnp.int16(off)
                lane = q & jnp.int16(LANES - 1)
                masks = [q >= jnp.int16(LANES * j) for j in range(1, 5)]
                got = [lane_gather(t, lane) for t in tiles]
                for start, weight in ((0, near), (4, beyond)):
                    value = got[start]
                    for j in range(4):
                        value = jnp.where(masks[j], got[start + j + 1], value)
                    term = weight[rows, cols] * value.astype(F32)
                    total = term if total is None else total + term
            adv[rows, cols] = total.astype(BF16)

    def columns(unit):
        right = (1 - core) if unit < 2 else core
        k = unit % 2
        block = right * (4 + 2 * k) + (1 - right) * (2 - 2 * k)
        return pl.ds(pl.multiple_of(block * LANES, 2 * LANES), 2 * LANES)

    def remote(src, dst, send, recv, peer):
        return pltpu.make_async_remote_copy(
            src_ref=src, dst_ref=dst, send_sem=send, recv_sem=recv, device_id={"lev": peer}, device_id_type=MESH
        )

    def partial_copy(unit, hop):
        return remote(
            part_tx.at[unit, hop], part_rx.at[unit, nlev - hop],
            part_send.at[unit, hop], part_recv.at[unit, nlev - hop], lax.rem(me + hop, nlev),
        )

    def middle_copy(unit, owner, hop):
        return remote(
            mid.at[unit, owner], mid.at[unit, owner], mid_send.at[unit, hop], mid_recv.at[unit, owner],
            lax.rem(owner + hop, nlev),
        )

    def quarter(peer):
        return pl.ds(pl.multiple_of(peer * QUARTER, QUARTER), QUARTER)

    def forward(unit):
        right = (1 - core) if unit < 2 else core
        for i in (2 * (unit % 2), 2 * (unit % 2) + 1):
            if unit >= 2:
                halo_copy(1 - right, i).wait_recv()
            elif i == 0:
                halo_copy(1 - right, 0, 4).wait_recv()
            advect(right * (4 + i) + (1 - right) * (3 - i))
        part[unit] = lax.dot_general(
            adv[:, columns(unit)], w1[...], (((0,), (0,)), ((), ())), preferred_element_type=F32
        )

    def send_partial(unit):
        for hop in (2, 1, 3):
            part_tx[unit, hop] = part[unit, quarter(lax.rem(me + hop, nlev)), :].astype(BF16)
            partial_copy(unit, hop).start()

    def complete(unit):
        total = part[unit, quarter(me), :] + bf_v[...]
        for hop in (1, 3, 2):
            partial_copy(unit, hop).wait_recv()
            total = total + part_rx[unit, nlev - hop].astype(F32)
        first = silu(total).astype(BF16)
        second = jnp.dot(first, wm_v[...], preferred_element_type=F32) + bm_v[...]
        mid[unit, me] = silu(second).astype(BF16)
        for hop in (2, 1, 3):
            middle_copy(unit, me, hop).start()

    def last(unit):
        for hop in (1, 3, 2):
            middle_copy(unit, lax.rem(me + hop, nlev), nlev - hop).wait_recv()
        cols = columns(unit)
        tendency = lax.dot_general(
            w3[...], mid[unit].reshape(2 * LANES, w3.shape[1]), (((1,), (1,)), ((), ())), preferred_element_type=F32
        )
        updated = (adv[:, cols].astype(F32) + tendency).astype(BF16)
        out[:, :, cols] = updated.reshape(levels, 8, 2 * LANES)

    forward(0)

    @pl.when(is_first)
    def _():
        pl.semaphore_wait(peers_in, nlev - 1)
        tell(lev_in, {"band": east})

    @pl.when(jnp.logical_not(is_first))
    def _():
        pl.semaphore_wait(lev_in, 1)

    send_partial(0)
    forward(1)
    send_partial(1)
    pl.when(ahead)(send_slow)
    forward(2)
    send_partial(2)
    forward(3)
    send_partial(3)
    for unit in range(4):
        complete(unit)
    for unit in range(4):
        last(unit)

    for unit in range(4):
        for hop in range(1, nlev):
            partial_copy(unit, hop).wait_send()
            middle_copy(unit, me, hop).wait_send()
    halo_copy(1 - core, 0, 4).wait_send()
    for i in range(4):
        halo_copy(core, i).wait_send()


def on_device(nband, nlev, fields, depart, fraction, w_first, b_first, w_middle, b_middle, w_last):
    nfield, levels, ncols = fields.shape
    nrow, hidden = nfield * levels, w_middle.shape[0]
    V, DMA = pltpu.VMEM, pltpu.SemaphoreType.DMA
    table = V((nrow, ncols), F32)
    window = V((nfield * WINDOW, hidden), BF16)
    operands = (
        fields.transpose(1, 0, 2),
        depart,
        fraction.transpose(1, 0, 2),
        w_first.reshape(-1, hidden),
        w_last.reshape(-1, hidden),
        w_middle,
        b_first[None, :],
        b_middle[None, :],
    )
    result = pl.pallas_call(
        functools.partial(kernel, nband, nlev),
        out_shape=jax.ShapeDtypeStruct((levels, nfield, ncols), BF16),
        in_specs=[pl.BlockSpec(memory_space=pltpu.HBM)] * 8,
        out_specs=pl.BlockSpec(memory_space=pltpu.VMEM),
        scratch_shapes=[
            V((levels, nfield, 2 * ncols), BF16),
            V((levels, ncols), jnp.int32),
            V((levels, 2, ncols), BF16),
            window,
            window,
            V((hidden, hidden), BF16),
            V((1, hidden), F32),
            V((1, hidden), F32),
            V((nrow, ncols), jnp.int16),
            table, table, table, table,
            V((nrow, ncols), BF16),
            V((nrow, hidden), BF16),
            V((nrow, hidden), BF16),
            V((4, 2 * LANES, hidden), F32),
            V((4, 4, QUARTER, hidden), BF16),
            V((4, 4, QUARTER, hidden), BF16),
            V((4, 4, QUARTER, hidden), BF16),
            DMA((22,)), DMA((2, 4)), DMA((2, 4)), DMA((4, 4)), DMA((4, 4)), DMA((4, 4)), DMA((4, 4)),
            pltpu.SemaphoreType.REGULAR, pltpu.SemaphoreType.REGULAR, pltpu.SemaphoreType.REGULAR,
        ],
        compiler_params=pltpu.CompilerParams(
            collective_id=0, has_side_effects=True, vmem_limit_bytes=40 << 20
        ),
    )(
        *(pltpu.with_memory_space_constraint(x, pltpu.HBM) for x in operands)
    )
    return result.transpose(1, 0, 2)


def solution(mesh):
    placed = (P(None, "lev", "band"), P("lev", "band"), P(None, "lev", "band"), P(), P(), P(), P(), P())
    return jax.shard_map(
        functools.partial(on_device, mesh.shape["band"], mesh.shape["lev"]),
        mesh=mesh,
        in_specs=placed,
        out_specs=P(None, "lev", "band"),
        check_vma=False,
    )
```

```python
import functools

import jax
import jax.numpy as jnp
from jax import lax
from jax.experimental import pallas as pl
from jax.experimental.pallas import tpu as pltpu
from jax.sharding import PartitionSpec as P

MESH = pl.DeviceIdType.MESH
F32, BF16 = jnp.float32, jnp.bfloat16
LANES = 128
WINDOW = 48
QUARTER = 32
BLOCKS = (2, 2, 2, 1, 1)
HALF = 2
STARTS = (0, 64, 128, 192, 224)
ROW = 512

_PICK = lax.GatherDimensionNumbers(
    offset_dims=(),
    collapsed_slice_dims=(1,),
    start_index_map=(1,),
    operand_batching_dims=(0,),
    start_indices_batching_dims=(0,),
)


def lane_gather(x, lane):
    return lax.gather(
        x, lane[..., None], _PICK, (1, 1), mode=lax.GatherScatterMode.PROMISE_IN_BOUNDS
    )


def silu(v):
    return v / (1.0 + jnp.exp(-v))


def kernel(
    nband, nlev, fields, depart, fraction, w_first, w_last, w_middle, b_first, b_middle, out,
    ext, dep_v, frac_v, wf_v, wl_v, wm_v, bf_v, bm_v, p16, w00, w01, w10, w11,
    adv, w1, w3, part, part_tx, part_rx, mid,
    load_sem, halo_send, halo_recv, part_send, part_recv, mid_send, mid_recv,
    west_in, peers_in, lev_in,
):
    band, me = lax.axis_index("band"), lax.axis_index("lev")
    nrow = adv.shape[0]
    levels = nrow // 8
    core = lax.rem(band, 2)
    east, west = lax.rem(band + 1, nband), lax.rem(band + nband - 1, nband)

    is_first = core == 0
    barrier = pltpu.get_barrier_semaphore()
    others = [lax.rem(me + hop, nlev) for hop in range(1, nlev)]

    def tell(sem, peer):
        pl.semaphore_signal(sem, inc=1, device_id=peer, device_id_type=MESH)

    @pl.when(is_first)
    def _():
        tell(barrier, {"band": west})
        tell(barrier, {"band": east})
        for peer in others:
            tell(barrier, {"lev": peer})

    place = lax.rem(band, 16)
    ahead, late = place == 0, place == 15
    greets_east, greeted = jnp.logical_and(core == 1, place != 15), jnp.logical_and(is_first, place != 0)

    @pl.when(jnp.logical_not(is_first))
    def _():
        tell(barrier, {"band": west})

    @pl.when(greets_east)
    def _():
        tell(barrier, {"band": east})

    pairs_of_refs = [(depart, dep_v), (fraction, frac_v), (fields, ext.at[:, :, pl.ds(ROW, 2 * ROW)])]
    for src, dst in ((w_first, wf_v), (w_last, wl_v)):
        for f in range(8):
            start = pl.multiple_of((f * nlev * levels + me * levels) // 16 * 16, 16)
            pairs_of_refs.append((src.at[pl.ds(start, WINDOW)], dst.at[pl.ds(f * WINDOW, WINDOW)]))
    pairs_of_refs += [(w_middle, wm_v), (b_first, bf_v), (b_middle, bm_v)]
    loads = [
        pltpu.make_async_copy(src, dst, load_sem.at[n]) for n, (src, dst) in enumerate(pairs_of_refs)
    ]
    def halo_copy(right, i, tiles=1):
        src = right * (8 - tiles - i) + (1 - right) * i
        dst = right * (4 - tiles - i) + (1 - right) * (12 + i)
        return pltpu.make_async_remote_copy(
            src_ref=fields.at[:, :, pl.ds(pl.multiple_of(src * LANES, LANES), tiles * LANES)],
            dst_ref=ext.at[:, :, pl.ds(pl.multiple_of(dst * LANES, LANES), tiles * LANES)],
            send_sem=halo_send.at[tiles // 4, i],
            recv_sem=halo_recv.at[tiles // 4, i],
            device_id={"band": right * east + (1 - right) * west},
            device_id_type=MESH,
        )

    def prepare(i, carry):
        lane = lax.rem(lax.broadcasted_iota(jnp.int32, (8, 2 * ROW), 1), LANES) + ROW
        where, weights = [], []
        for j in range(2):
            level = 2 * i + j
            where.append(lane + jnp.broadcast_to(dep_v[pl.ds(level, 1), :], (8, 2 * ROW)))
            both = frac_v[level].astype(F32)
            a = jnp.broadcast_to(both[0:1], (8, 2 * ROW))
            b = jnp.broadcast_to(both[1:2], (8, 2 * ROW))
            weights.append(((1.0 - a) * (1.0 - b), a * (1.0 - b), (1.0 - a) * b, a * b))
        rows = pl.ds(pl.multiple_of(16 * i, 16), 16)
        p16[rows, :] = jnp.concatenate(where, axis=0).astype(jnp.int16)
        for ref, one, two in zip((w00, w01, w10, w11), *weights):
            ref[rows, :] = jnp.concatenate([one, two], axis=0)
        return carry

    def send_slow():
        for i, tiles in ((0, 2), (2, 1), (3, 1)):
            halo_copy(core, i, tiles).start()

    def answer_west():
        pl.semaphore_wait(west_in, 1)
        send_slow()

    def start_loads():
        for load in loads:
            load.start()

    pl.when(jnp.logical_not(late))(start_loads)

    @pl.when(jnp.logical_not(is_first))
    def _():
        pl.semaphore_wait(barrier, 2)

        @pl.when(jnp.logical_not(greets_east))
        def _():
            tell(west_in, {"band": east})

        send_slow()
        halo_copy(1 - core, 0, 4).start()

    pl.when(late)(start_loads)

    @pl.when(is_first)
    def _():
        @pl.when(greeted)
        def _():
            pl.semaphore_wait(barrier, nlev + 1)
            send_slow()

        @pl.when(ahead)
        def _():
            pl.semaphore_wait(barrier, nlev)

        for peer in others:
            tell(peers_in, {"lev": peer})
        halo_copy(1 - core, 0, 4).start()

    loads[0].wait()
    loads[1].wait()
    lax.fori_loop(0, levels // 2, prepare, 0)

    for load in loads[3:]:
        load.wait()
    r = lax.broadcasted_iota(jnp.int32, (nrow, 8 * WINDOW), 0)
    field = r & 7
    source = field * WINDOW + (field & 1) * 8 + me * 2 + (r >> 3)
    pick = jnp.where(lax.broadcasted_iota(jnp.int32, (nrow, 8 * WINDOW), 1) == source, 1.0, 0.0).astype(BF16)
    w1[...] = jnp.dot(pick, wf_v[...], preferred_element_type=F32).astype(BF16)
    w3[...] = jnp.dot(pick, wl_v[...], preferred_element_type=F32).astype(BF16)
    loads[2].wait()

    def advect(block):
        base = block * LANES
        cols = slice(base, base + LANES)

        for g in range(nrow // 16):
            rows = slice(16 * g, 16 * g + 16)
            p = p16[rows, cols]
            tiles = [
                ext[2 * g : 2 * g + 2, :, base + LANES * t : base + LANES * (t + 1)].reshape(16, LANES) for t in range(9)
            ]
            total = None
            for off, near, beyond in ((0, w00, w10), (1, w01, w11)):
                q = p + jnp.int16(off)
                lane = q & jnp.int16(LANES - 1)
                masks = [q >= jnp.int16(LANES * j) for j in range(1, 5)]
                got = [lane_gather(t, lane) for t in tiles]
                for start, weight in ((0, near), (4, beyond)):
                    value = got[start]
                    for j in range(4):
                        value = jnp.where(masks[j], got[start + j + 1], value)
                    term = weight[rows, cols] * value.astype(F32)
                    total = term if total is None else total + term
            adv[rows, cols] = total.astype(BF16)

    def first_block(this_core, unit):
        before = sum(BLOCKS[:unit]) % 4
        right = (1 - this_core) if unit < HALF else this_core
        return right * (4 + before) + (1 - right) * (4 - before - BLOCKS[unit])

    def columns(unit):
        return pl.ds(pl.multiple_of(first_block(core, unit) * LANES, LANES), BLOCKS[unit] * LANES)

    def rows_of(unit):
        return pl.ds(STARTS[unit], BLOCKS[unit] * QUARTER)

    def remote(src, dst, send, recv, peer):
        return pltpu.make_async_remote_copy(
            src_ref=src, dst_ref=dst, send_sem=send, recv_sem=recv, device_id={"lev": peer}, device_id_type=MESH
        )

    def partial_copy(unit, hop):
        return remote(
            part_tx.at[hop, rows_of(unit)], part_rx.at[nlev - hop, rows_of(unit)],
            part_send.at[unit, hop], part_recv.at[unit, nlev - hop], lax.rem(me + hop, nlev),
        )

    def middle_copy(unit, owner, hop):
        return remote(
            mid.at[owner, rows_of(unit)], mid.at[owner, rows_of(unit)], mid_send.at[unit, hop], mid_recv.at[unit, owner],
            lax.rem(owner + hop, nlev),
        )

    def quarter(unit, peer):
        size = BLOCKS[unit] * QUARTER
        return pl.ds(pl.multiple_of(first_block(core, unit) * LANES + peer * size, size), size)

    def forward_on(this_core, unit):
        first = first_block(this_core, unit)
        for block in range(first, first + BLOCKS[unit]):
            advect(block)
        cols = slice(first * LANES, (first + BLOCKS[unit]) * LANES)
        part[cols, :] = lax.dot_general(
            adv[:, cols], w1[...], (((0,), (0,)), ((), ())), preferred_element_type=F32
        )

    def forward(unit):
        if unit == 0:
            halo_copy(core, 0, 4).wait_recv()
        elif unit >= HALF:
            halo_copy(1 - core, sum(BLOCKS[HALF:unit]), BLOCKS[unit]).wait_recv()
        pl.when(is_first)(functools.partial(forward_on, 0, unit))
        pl.when(jnp.logical_not(is_first))(functools.partial(forward_on, 1, unit))

    def send_partial(unit):
        for hop in (2, 1, 3):
            part_tx[hop, rows_of(unit), :] = part[quarter(unit, lax.rem(me + hop, nlev)), :].astype(BF16)
            partial_copy(unit, hop).start()

    def complete(unit):
        total = part[quarter(unit, me), :] + bf_v[...]
        for hop in (1, 3, 2):
            partial_copy(unit, hop).wait_recv()
            total = total + part_rx[nlev - hop, rows_of(unit), :].astype(F32)
        first = silu(total).astype(BF16)
        second = jnp.dot(first, wm_v[...], preferred_element_type=F32) + bm_v[...]
        mid[me, rows_of(unit), :] = silu(second).astype(BF16)
        for hop in (2, 1, 3):
            middle_copy(unit, me, hop).start()

    def last(unit):
        for hop in (1, 3, 2):
            middle_copy(unit, lax.rem(me + hop, nlev), nlev - hop).wait_recv()
        cols = columns(unit)
        width = BLOCKS[unit] * LANES
        tendency = lax.dot_general(
            w3[...], mid[:, rows_of(unit), :].reshape(width, w3.shape[1]), (((1,), (1,)), ((), ())),
            preferred_element_type=F32,
        )
        updated = (adv[:, cols].astype(F32) + tendency).astype(BF16)
        out[:, :, cols] = updated.reshape(levels, 8, width)

    forward(0)

    @pl.when(is_first)
    def _():
        pl.semaphore_wait(peers_in, nlev - 1)
        tell(lev_in, {"band": east})

    @pl.when(jnp.logical_not(is_first))
    def _():
        pl.semaphore_wait(lev_in, 1)

    send_partial(0)
    for unit in range(1, len(BLOCKS)):
        if unit == HALF:
            pl.when(ahead)(answer_west)
        forward(unit)
        send_partial(unit)
    for unit in range(len(BLOCKS)):
        complete(unit)
    for unit in range(len(BLOCKS)):
        last(unit)

    for unit in range(len(BLOCKS)):
        for hop in range(1, nlev):
            partial_copy(unit, hop).wait_send()
            middle_copy(unit, me, hop).wait_send()
    halo_copy(1 - core, 0, 4).wait_send()
    for i, tiles in ((0, 2), (2, 1), (3, 1)):
        halo_copy(core, i, tiles).wait_send()


def on_device(nband, nlev, fields, depart, fraction, w_first, b_first, w_middle, b_middle, w_last):
    nfield, levels, ncols = fields.shape
    nrow, hidden = nfield * levels, w_middle.shape[0]
    V, DMA = pltpu.VMEM, pltpu.SemaphoreType.DMA
    table = V((nrow, ncols), F32)
    window = V((nfield * WINDOW, hidden), BF16)
    operands = (
        fields.transpose(1, 0, 2),
        depart,
        fraction.transpose(1, 0, 2),
        w_first.reshape(-1, hidden),
        w_last.reshape(-1, hidden),
        w_middle,
        b_first[None, :],
        b_middle[None, :],
    )
    result = pl.pallas_call(
        functools.partial(kernel, nband, nlev),
        out_shape=jax.ShapeDtypeStruct((levels, nfield, ncols), BF16),
        in_specs=[pl.BlockSpec(memory_space=pltpu.HBM)] * 8,
        out_specs=pl.BlockSpec(memory_space=pltpu.VMEM),
        scratch_shapes=[
            V((levels, nfield, 2 * ncols), BF16),
            V((levels, ncols), jnp.int32),
            V((levels, 2, ncols), BF16),
            window,
            window,
            V((hidden, hidden), BF16),
            V((1, hidden), F32),
            V((1, hidden), F32),
            V((nrow, ncols), jnp.int16),
            table, table, table, table,
            V((nrow, ncols), BF16),
            V((nrow, hidden), BF16),
            V((nrow, hidden), BF16),
            V((ncols, hidden), F32),
            V((4, ncols // 4, hidden), BF16),
            V((4, ncols // 4, hidden), BF16),
            V((4, ncols // 4, hidden), BF16),
            DMA((22,)), DMA((2, 4)), DMA((2, 4)), DMA((5, 4)), DMA((5, 4)), DMA((5, 4)), DMA((5, 4)),
            pltpu.SemaphoreType.REGULAR, pltpu.SemaphoreType.REGULAR, pltpu.SemaphoreType.REGULAR,
        ],
        compiler_params=pltpu.CompilerParams(
            collective_id=0, has_side_effects=True, vmem_limit_bytes=40 << 20
        ),
    )(
        *(pltpu.with_memory_space_constraint(x, pltpu.HBM) for x in operands)
    )
    return result.transpose(1, 0, 2)


def solution(mesh):
    placed = (P(None, "lev", "band"), P("lev", "band"), P(None, "lev", "band"), P(), P(), P(), P(), P())
    return jax.shard_map(
        functools.partial(on_device, mesh.shape["band"], mesh.shape["lev"]),
        mesh=mesh,
        in_specs=placed,
        out_specs=P(None, "lev", "band"),
        check_vma=False,
    )
```

```python
import functools

import jax
import jax.numpy as jnp
from jax import lax
from jax.experimental import pallas as pl
from jax.experimental.pallas import tpu as pltpu
from jax.sharding import PartitionSpec as P

MESH = pl.DeviceIdType.MESH
F32, BF16 = jnp.float32, jnp.bfloat16
LANES = 128
WINDOW = 48
QUARTER = 32
BLOCKS = (2, 2, 2, 1, 1)
HALF = 2
STARTS = (0, 64, 128, 192, 224)
ROW = 512

_PICK = lax.GatherDimensionNumbers(
    offset_dims=(),
    collapsed_slice_dims=(1,),
    start_index_map=(1,),
    operand_batching_dims=(0,),
    start_indices_batching_dims=(0,),
)


def lane_gather(x, lane):
    return lax.gather(
        x, lane[..., None], _PICK, (1, 1), mode=lax.GatherScatterMode.PROMISE_IN_BOUNDS
    )


def silu(v):
    return v / (1.0 + jnp.exp(-v))


def kernel(
    nband, nlev, fields, depart, fraction, w_first, w_last, w_middle, b_first, b_middle, out,
    ext, dep_v, frac_v, wf_v, wl_v, wm_v, bf_v, bm_v, p16, w00, w01, w10, w11,
    adv, w1, w3, part, part_tx, part_rx, mid,
    load_sem, halo_send, halo_recv, part_send, part_recv, mid_send, mid_recv,
    west_in, peers_in, lev_in,
):
    band, me = lax.axis_index("band"), lax.axis_index("lev")
    nrow = adv.shape[0]
    levels = nrow // 8
    core = lax.rem(band, 2)
    east, west = lax.rem(band + 1, nband), lax.rem(band + nband - 1, nband)

    is_first = core == 0
    barrier = pltpu.get_barrier_semaphore()
    others = [lax.rem(me + hop, nlev) for hop in range(1, nlev)]

    def tell(sem, peer):
        pl.semaphore_signal(sem, inc=1, device_id=peer, device_id_type=MESH)

    @pl.when(is_first)
    def _():
        tell(barrier, {"band": west})
        tell(barrier, {"band": east})
        for peer in others:
            tell(barrier, {"lev": peer})

    place = lax.rem(band, 16)
    ahead, late = place == 0, place == 15
    greets_east, greeted = jnp.logical_and(core == 1, place != 15), jnp.logical_and(is_first, place != 0)

    @pl.when(jnp.logical_not(is_first))
    def _():
        tell(barrier, {"band": west})

    @pl.when(greets_east)
    def _():
        tell(barrier, {"band": east})

    pairs_of_refs = [(depart, dep_v), (fraction, frac_v), (fields, ext.at[:, :, pl.ds(ROW, 2 * ROW)])]
    for src, dst in ((w_first, wf_v), (w_last, wl_v)):
        for f in range(8):
            start = pl.multiple_of((f * nlev * levels + me * levels) // 16 * 16, 16)
            pairs_of_refs.append((src.at[pl.ds(start, WINDOW)], dst.at[pl.ds(f * WINDOW, WINDOW)]))
    pairs_of_refs += [(w_middle, wm_v), (b_first, bf_v), (b_middle, bm_v)]
    loads = [
        pltpu.make_async_copy(src, dst, load_sem.at[n]) for n, (src, dst) in enumerate(pairs_of_refs)
    ]
    def halo_copy(right, i, tiles=1):
        src = right * (8 - tiles - i) + (1 - right) * i
        dst = right * (4 - tiles - i) + (1 - right) * (12 + i)
        return pltpu.make_async_remote_copy(
            src_ref=fields.at[:, :, pl.ds(pl.multiple_of(src * LANES, LANES), tiles * LANES)],
            dst_ref=ext.at[:, :, pl.ds(pl.multiple_of(dst * LANES, LANES), tiles * LANES)],
            send_sem=halo_send.at[tiles // 4, i],
            recv_sem=halo_recv.at[tiles // 4, i],
            device_id={"band": right * east + (1 - right) * west},
            device_id_type=MESH,
        )

    def prepare(i, carry):
        lane = lax.rem(lax.broadcasted_iota(jnp.int32, (8, 2 * ROW), 1), LANES) + ROW
        where, weights = [], []
        for j in range(2):
            level = 2 * i + j
            where.append(lane + jnp.broadcast_to(dep_v[pl.ds(level, 1), :], (8, 2 * ROW)))
            both = frac_v[level].astype(F32)
            a = jnp.broadcast_to(both[0:1], (8, 2 * ROW))
            b = jnp.broadcast_to(both[1:2], (8, 2 * ROW))
            weights.append(((1.0 - a) * (1.0 - b), a * (1.0 - b), (1.0 - a) * b, a * b))
        rows = pl.ds(pl.multiple_of(16 * i, 16), 16)
        p16[rows, :] = jnp.concatenate(where, axis=0).astype(jnp.int16)
        for ref, one, two in zip((w00, w01, w10, w11), *weights):
            ref[rows, :] = jnp.concatenate([one, two], axis=0)
        return carry

    def send_slow():
        for i, tiles in ((0, 2), (2, 1), (3, 1)):
            halo_copy(core, i, tiles).start()

    def answer_west():
        pl.semaphore_wait(west_in, 1)
        send_slow()

    def start_loads():
        for load in loads:
            load.start()

    pl.when(jnp.logical_not(late))(start_loads)

    @pl.when(jnp.logical_not(is_first))
    def _():
        pl.semaphore_wait(barrier, 2)

        @pl.when(jnp.logical_not(greets_east))
        def _():
            tell(west_in, {"band": east})

        halo_copy(1 - core, 0, 4).start()
        send_slow()

    pl.when(late)(start_loads)

    @pl.when(is_first)
    def _():
        @pl.when(greeted)
        def _():
            pl.semaphore_wait(barrier, nlev + 1)

        @pl.when(ahead)
        def _():
            pl.semaphore_wait(barrier, nlev)

        for peer in others:
            tell(peers_in, {"lev": peer})
        halo_copy(1 - core, 0, 4).start()
        pl.when(greeted)(send_slow)

    loads[0].wait()
    loads[1].wait()
    lax.fori_loop(0, levels // 2, prepare, 0)

    for load in loads[3:]:
        load.wait()
    r = lax.broadcasted_iota(jnp.int32, (nrow, 8 * WINDOW), 0)
    field = r & 7
    source = field * WINDOW + (field & 1) * 8 + me * 2 + (r >> 3)
    pick = jnp.where(lax.broadcasted_iota(jnp.int32, (nrow, 8 * WINDOW), 1) == source, 1.0, 0.0).astype(BF16)
    w1[...] = jnp.dot(pick, wf_v[...], preferred_element_type=F32).astype(BF16)
    w3[...] = jnp.dot(pick, wl_v[...], preferred_element_type=F32).astype(BF16)
    loads[2].wait()

    def advect(block):
        base = block * LANES
        cols = slice(base, base + LANES)

        for g in range(nrow // 16):
            rows = slice(16 * g, 16 * g + 16)
            p = p16[rows, cols]
            tiles = [
                ext[2 * g : 2 * g + 2, :, base + LANES * t : base + LANES * (t + 1)].reshape(16, LANES) for t in range(9)
            ]
            total = None
            for off, near, beyond in ((0, w00, w10), (1, w01, w11)):
                q = p + jnp.int16(off)
                lane = q & jnp.int16(LANES - 1)
                masks = [q >= jnp.int16(LANES * j) for j in range(1, 5)]
                got = [lane_gather(t, lane) for t in tiles]
                for start, weight in ((0, near), (4, beyond)):
                    value = got[start]
                    for j in range(4):
                        value = jnp.where(masks[j], got[start + j + 1], value)
                    term = weight[rows, cols] * value.astype(F32)
                    total = term if total is None else total + term
            adv[rows, cols] = total.astype(BF16)

    def first_block(this_core, unit):
        before = sum(BLOCKS[:unit]) % 4
        right = (1 - this_core) if unit < HALF else this_core
        return right * (4 + before) + (1 - right) * (4 - before - BLOCKS[unit])

    def columns(unit):
        return pl.ds(pl.multiple_of(first_block(core, unit) * LANES, LANES), BLOCKS[unit] * LANES)

    def rows_of(unit):
        return pl.ds(STARTS[unit], BLOCKS[unit] * QUARTER)

    def remote(src, dst, send, recv, peer):
        return pltpu.make_async_remote_copy(
            src_ref=src, dst_ref=dst, send_sem=send, recv_sem=recv, device_id={"lev": peer}, device_id_type=MESH
        )

    def partial_copy(unit, hop):
        return remote(
            part_tx.at[hop, rows_of(unit)], part_rx.at[nlev - hop, rows_of(unit)],
            part_send.at[unit, hop], part_recv.at[unit, nlev - hop], lax.rem(me + hop, nlev),
        )

    def middle_copy(unit, owner, hop):
        return remote(
            mid.at[owner, rows_of(unit)], mid.at[owner, rows_of(unit)], mid_send.at[unit, hop], mid_recv.at[unit, owner],
            lax.rem(owner + hop, nlev),
        )

    def quarter(unit, peer):
        size = BLOCKS[unit] * QUARTER
        return pl.ds(pl.multiple_of(first_block(core, unit) * LANES + peer * size, size), size)

    def forward_on(this_core, unit):
        first = first_block(this_core, unit)
        for block in range(first, first + BLOCKS[unit]):
            advect(block)
        cols = slice(first * LANES, (first + BLOCKS[unit]) * LANES)
        part[cols, :] = lax.dot_general(
            adv[:, cols], w1[...], (((0,), (0,)), ((), ())), preferred_element_type=F32
        )

    def forward(unit):
        if unit == 0:
            halo_copy(core, 0, 4).wait_recv()
        elif unit >= HALF:
            halo_copy(1 - core, sum(BLOCKS[HALF:unit]), BLOCKS[unit]).wait_recv()
        pl.when(is_first)(functools.partial(forward_on, 0, unit))
        pl.when(jnp.logical_not(is_first))(functools.partial(forward_on, 1, unit))

    def send_partial(unit):
        for hop in (2, 1, 3):
            part_tx[hop, rows_of(unit), :] = part[quarter(unit, lax.rem(me + hop, nlev)), :].astype(BF16)
            partial_copy(unit, hop).start()

    def complete(unit):
        total = part[quarter(unit, me), :] + bf_v[...]
        for hop in (1, 3, 2):
            partial_copy(unit, hop).wait_recv()
            total = total + part_rx[nlev - hop, rows_of(unit), :].astype(F32)
        first = silu(total).astype(BF16)
        second = jnp.dot(first, wm_v[...], preferred_element_type=F32) + bm_v[...]
        mid[me, rows_of(unit), :] = silu(second).astype(BF16)
        for hop in (2, 1, 3):
            middle_copy(unit, me, hop).start()

    def last(unit):
        for hop in (1, 3, 2):
            middle_copy(unit, lax.rem(me + hop, nlev), nlev - hop).wait_recv()
        cols = columns(unit)
        width = BLOCKS[unit] * LANES
        tendency = lax.dot_general(
            w3[...], mid[:, rows_of(unit), :].reshape(width, w3.shape[1]), (((1,), (1,)), ((), ())),
            preferred_element_type=F32,
        )
        updated = (adv[:, cols].astype(F32) + tendency).astype(BF16)
        out[:, :, cols] = updated.reshape(levels, 8, width)

    forward(0)

    @pl.when(is_first)
    def _():
        pl.semaphore_wait(peers_in, nlev - 1)
        tell(lev_in, {"band": east})

    @pl.when(jnp.logical_not(is_first))
    def _():
        pl.semaphore_wait(lev_in, 1)

    send_partial(0)
    for unit in range(1, len(BLOCKS)):
        if unit == HALF:
            pl.when(ahead)(answer_west)
        forward(unit)
        send_partial(unit)
    for unit in range(len(BLOCKS)):
        complete(unit)
    for unit in range(len(BLOCKS)):
        last(unit)

    for unit in range(len(BLOCKS)):
        for hop in range(1, nlev):
            partial_copy(unit, hop).wait_send()
            middle_copy(unit, me, hop).wait_send()
    halo_copy(1 - core, 0, 4).wait_send()
    for i, tiles in ((0, 2), (2, 1), (3, 1)):
        halo_copy(core, i, tiles).wait_send()


def on_device(nband, nlev, fields, depart, fraction, w_first, b_first, w_middle, b_middle, w_last):
    nfield, levels, ncols = fields.shape
    nrow, hidden = nfield * levels, w_middle.shape[0]
    V, DMA = pltpu.VMEM, pltpu.SemaphoreType.DMA
    table = V((nrow, ncols), F32)
    window = V((nfield * WINDOW, hidden), BF16)
    operands = (
        fields.transpose(1, 0, 2),
        depart,
        fraction.transpose(1, 0, 2),
        w_first.reshape(-1, hidden),
        w_last.reshape(-1, hidden),
        w_middle,
        b_first[None, :],
        b_middle[None, :],
    )
    result = pl.pallas_call(
        functools.partial(kernel, nband, nlev),
        out_shape=jax.ShapeDtypeStruct((levels, nfield, ncols), BF16),
        in_specs=[pl.BlockSpec(memory_space=pltpu.HBM)] * 8,
        out_specs=pl.BlockSpec(memory_space=pltpu.VMEM),
        scratch_shapes=[
            V((levels, nfield, 2 * ncols), BF16),
            V((levels, ncols), jnp.int32),
            V((levels, 2, ncols), BF16),
            window,
            window,
            V((hidden, hidden), BF16),
            V((1, hidden), F32),
            V((1, hidden), F32),
            V((nrow, ncols), jnp.int16),
            table, table, table, table,
            V((nrow, ncols), BF16),
            V((nrow, hidden), BF16),
            V((nrow, hidden), BF16),
            V((ncols, hidden), F32),
            V((4, ncols // 4, hidden), BF16),
            V((4, ncols // 4, hidden), BF16),
            V((4, ncols // 4, hidden), BF16),
            DMA((22,)), DMA((2, 4)), DMA((2, 4)), DMA((5, 4)), DMA((5, 4)), DMA((5, 4)), DMA((5, 4)),
            pltpu.SemaphoreType.REGULAR, pltpu.SemaphoreType.REGULAR, pltpu.SemaphoreType.REGULAR,
        ],
        compiler_params=pltpu.CompilerParams(
            collective_id=0, has_side_effects=True, vmem_limit_bytes=40 << 20
        ),
    )(
        *(pltpu.with_memory_space_constraint(x, pltpu.HBM) for x in operands)
    )
    return result.transpose(1, 0, 2)


def solution(mesh):
    placed = (P(None, "lev", "band"), P("lev", "band"), P(None, "lev", "band"), P(), P(), P(), P(), P())
    return jax.shard_map(
        functools.partial(on_device, mesh.shape["band"], mesh.shape["lev"]),
        mesh=mesh,
        in_specs=placed,
        out_specs=P(None, "lev", "band"),
        check_vma=False,
    )
```
